512 devices in a mesh: row: 32 (over y, x), col: 16 (over z, core).
Axes of the slice: x: 4, y: 8, z: 8, core: 2. Of those that a mesh axis runs over, the one named last changes fastest.
Arguments:
- inputs: bfloat16 [2048, 16384], P('col', 'row'), may hold values from -6 to 6
- out_grad: bfloat16 [2048, 16384], P('col', 'row'), may hold values from -6 to 6
- gate_pre: bfloat16 [2048, 6656], P('row', 'col'), may hold values from -6 to 6
- up_pre: bfloat16 [2048, 6656], P('row', 'col'), may hold values from -6 to 6
- w_gate: bfloat16 [16384, 6656], P('row', 'col'), may hold values from -0.046875 to 0.046875
- w_up: bfloat16 [16384, 6656], P('row', 'col'), may hold values from -0.046875 to 0.046875
- w_down: bfloat16 [6656, 16384], P('col', 'row'), may hold values from -0.078125 to 0.078125
- segment_ids: int32 [2048], P('col'), may hold values from 0 to 63, never falling along the last dimension, each value on 1 to 64 neighbouring positions
Outputs:
- in_grad: bfloat16 [2048, 16384], P('col', 'row')
- grad_gate: bfloat16 [16384, 6656], P('row', 'col')
- grad_up: bfloat16 [16384, 6656], P('row', 'col')
- grad_down: bfloat16 [6656, 16384], P('col', 'row')
The draws below stay inside these ranges and needn't reach their ends.
Inputs may be any that keep to these rules, and one draw needn't show every extreme that they name: `segment_ids`: ids never fall along the tokens; every id from 0 up to the largest occurs; odd ids mark tool-result documents.
All inputs are finite; a program needn't handle non-finite values.
Results may differ from the reference program's by a relative error of at most 0.033.
Values may be sent and summed in bfloat16 or wider, within the bound.
No kernel may reach another device: no remote copies, remote signals or barrier semaphores. Data moves between devices by JAX's collectives and lax.ppermute only.
A program may use at most 64 MiB of HBM per device.

```python
import math
import jax
import jax.numpy as jnp
import numpy as np
from jax import lax

D = 16384
FF = 6656
TOKENS = 2048
N_ROW = 32
N_COL = 16


def spiked(drawn, own_key, source, target, shards_of, factor):
    def block_of(position):
        return (jnp.arange(drawn.shape[position]) // (drawn.shape[position] // shards_of)).reshape((-1,) + (1,) * (drawn.ndim - 1 - position))

    first = jax.random.permutation(own_key, shards_of)[block_of(target)]
    other_side = (block_of(target) + shards_of // 2) % shards_of
    return jnp.where((block_of(source) == first) | (block_of(source) == other_side), factor * drawn, drawn)


def shard_levels(own_key, shape, pieces, low, high):
    gain, own = 1.0, jax.random.fold_in(own_key, 6)
    for position, shards_of in pieces:
        draws = jnp.exp(jax.random.uniform(jax.random.fold_in(own, position), (shards_of,), jnp.float32, low / len(pieces), high / len(pieces)))
        gain = gain * jnp.repeat(draws, shape[position] // shards_of).reshape([-1 if axis == position else 1 for axis in range(len(shape))])
    return gain


def profile(amount, total, most, slope):
    weights = [(1 << 20) // math.isqrt(standing ** slope) + 1 for standing in range(2, amount + 1)]
    surplus, given = total - most - (amount - 1), [1] * (amount - 1)
    while surplus > 0:
        movable = [i for i in range(amount - 1) if given[i] < most]
        mass, budget = sum([weights[i] for i in movable]), surplus
        for i in movable:
            more = min(most - given[i], max(1, budget * weights[i] // mass), surplus)
            given[i] = given[i] + more
            surplus = surplus - more
    return np.array([most] + given)


def uneven(key, count, total, limit, skew):
    if count == 2:
        one = jax.random.randint(key, (), max(1, total - limit), min(limit, total - 1) + 1)
        return jnp.stack([one, total - one])
    tallies = jnp.asarray(profile(count, total, limit, skew), jnp.int32)
    twos = (count - 1) // 2
    source_of, sink = tallies[1:1 + 2 * twos:2], tallies[2:2 + 2 * twos:2]
    room = jnp.minimum(source_of - 1, limit - sink)
    passed = jax.random.randint(jax.random.fold_in(key, 1), (twos,), 0, 1 << 20) % (room + 1)
    tallies = tallies.at[1:1 + 2 * twos:2].set(source_of - passed).at[2:2 + 2 * twos:2].set(sink + passed)
    return tallies[jax.random.permutation(jax.random.fold_in(key, 2), count)]


def noise(rng, shape, spread, limit, pieces=(), kind=jnp.bfloat16):
    values = jax.random.normal(rng, shape, jnp.float32) * spread
    if len(pieces) > 0:
        values = shard_levels(rng, shape, pieces, -0.22, 0.18) * values
    return jnp.clip(values, min=-limit, max=limit).astype(kind)


def heavy_noise(key, extent, deviation, limit, cuts, heavy, kind=jnp.bfloat16):
    values = deviation * jax.random.normal(key, extent, jnp.float32)
    if cuts:
        values = values * shard_levels(key, extent, cuts, -0.22, 0.18)
    return jnp.clip(spiked(values, jax.random.fold_in(key, 3), *heavy), -limit, limit).astype(kind)


def setup_inputs(seed: int = 0) -> dict:
    key_list = jax.random.split(jax.random.key(seed), 9)
    inputs = noise(key_list[0], (TOKENS, D), 1.0, 6.0, ((0, 16), (1, 32)))
    out_grad = heavy_noise(key_list[1], (TOKENS, D), 1.0, 6.0, ((0, 16), (1, 32)), (1, 0, 32, 2.75))
    gate_pre = noise(key_list[2], (TOKENS, FF), 1.0, 6.0, ((0, 32), (1, 16)))
    up_pre = noise(key_list[3], (TOKENS, FF), 1.0, 6.0, ((0, 32), (1, 16)))
    w_gate = noise(key_list[4], (D, FF), D ** -0.5, 0.046875, ((0, 32), (1, 16)))
    w_up = noise(key_list[5], (D, FF), D ** -0.5, 0.046875, ((0, 32), (1, 16)))
    w_down = noise(key_list[6], (FF, D), FF ** -0.5, 0.078125, ((0, 16), (1, 32)))
    segment_ids = jnp.searchsorted(jnp.cumsum(uneven(key_list[7], max(2, TOKENS // 32), TOKENS, min(64, TOKENS), 0)), jnp.arange(TOKENS), side="right").astype(jnp.int32)
    return {"inputs": inputs, "out_grad": out_grad, "gate_pre": gate_pre, "up_pre": up_pre, "w_gate": w_gate, "w_up": w_up, "w_down": w_down, "segment_ids": segment_ids}


def block_sum(left, right, width, blocks):
    def step(total, index):
        start = (index * width).astype(jnp.int32)
        piece_left = lax.dynamic_slice_in_dim(left, start, width, 1)
        piece_right = lax.dynamic_slice_in_dim(right, start, width, 1)
        part = jnp.dot(piece_left, piece_right.T, preferred_element_type=jnp.float32)
        rounded = lax.optimization_barrier(part.astype(jnp.bfloat16))
        return total + rounded.astype(jnp.float32), None
    start_total = jnp.zeros((left.shape[0], right.shape[0]), jnp.float32)
    total, unused = lax.scan(step, start_total, jnp.arange(blocks, dtype=jnp.int32))
    return total


def reference(inputs, out_grad, gate_pre, up_pre, w_gate, w_up, w_down, segment_ids):
    keep = (segment_ids % 2 == 1).astype(jnp.bfloat16)
    masked = out_grad * keep[:, None]
    masked_wide = masked.astype(jnp.float32)
    hidden_grad = block_sum(masked_wide, w_down.astype(jnp.float32), D // N_ROW, N_ROW)
    gate = gate_pre.astype(jnp.float32)
    up = up_pre.astype(jnp.float32)
    sig = jax.nn.sigmoid(gate)
    silu = gate * sig
    hidden = (silu * up).astype(jnp.bfloat16)
    gate_grad = (hidden_grad * up * sig * (1.0 + gate * (1.0 - sig))).astype(jnp.bfloat16)
    up_grad = (hidden_grad * silu).astype(jnp.bfloat16)
    both_grads = jnp.concatenate([gate_grad.astype(jnp.float32), up_grad.astype(jnp.float32)], axis=1)
    width = FF // N_COL
    gate_wide = w_gate.astype(jnp.float32)
    up_wide = w_up.astype(jnp.float32)
    both_weights = jnp.concatenate([gate_wide, up_wide], axis=1)

    def step(total, index):
        start = (index * width).astype(jnp.int32)
        grads_gate = lax.dynamic_slice_in_dim(both_grads, start, width, 1)
        grads_up = lax.dynamic_slice_in_dim(both_grads, start + FF, width, 1)
        weights_gate = lax.dynamic_slice_in_dim(both_weights, start, width, 1)
        weights_up = lax.dynamic_slice_in_dim(both_weights, start + FF, width, 1)
        part = jnp.dot(grads_gate, weights_gate.T, preferred_element_type=jnp.float32)
        part = part + jnp.dot(grads_up, weights_up.T, preferred_element_type=jnp.float32)
        rounded = lax.optimization_barrier(part.astype(jnp.bfloat16))
        return total + rounded.astype(jnp.float32), None
    zeros_start = jnp.zeros((TOKENS, D), jnp.float32)
    input_total, unused = lax.scan(step, zeros_start, jnp.arange(N_COL, dtype=jnp.int32))
    in_grad = input_total.astype(jnp.bfloat16)
    scale = TOKENS ** -0.5
    inputs_wide = inputs.astype(jnp.float32)
    grad_gate = (jnp.dot(inputs_wide.T, gate_grad.astype(jnp.float32), preferred_element_type=jnp.float32) * scale).astype(jnp.bfloat16)
    grad_up = (jnp.dot(inputs_wide.T, up_grad.astype(jnp.float32), preferred_element_type=jnp.float32) * scale).astype(jnp.bfloat16)
    grad_down = (jnp.dot(hidden.astype(jnp.float32).T, masked_wide, preferred_element_type=jnp.float32) * scale).astype(jnp.bfloat16)
    return in_grad, grad_gate, grad_up, grad_down
```

```python
import jax
import jax.numpy as jnp
from jax import lax
from jax.sharding import Mesh, PartitionSpec as P

BF = jnp.bfloat16
F32 = jnp.float32


def tied(value, other):
    return lax.optimization_barrier((value, other))[0]


def make_body(ny, nx, nz):
    def shift_x(v, s):
        return lax.ppermute(v, "x", [(i, (i + s) % nx) for i in range(nx)])

    def swap_core(v):
        return lax.ppermute(v, "core", [(0, 1), (1, 0)])

    def body(inputs, out_grad, gate_pre, up_pre, w_gate, w_up, w_down, segment_ids):
        x, core = lax.axis_index("x"), lax.axis_index("core")
        tokens, width = inputs.shape
        units = w_down.shape[0]
        part = tokens // nx
        total = tokens * nz * 2
        scale = total ** (-0.5)

        def place_x(blocks, axis):
            shape = list(blocks[0].shape)
            shape.insert(axis, nx)
            out = jnp.zeros(shape, blocks[0].dtype)
            for s, block in enumerate(blocks):
                out = lax.dynamic_update_slice_in_dim(
                    out, jnp.expand_dims(block, axis), (x - s) % nx, axis
                )
            return out

        def gather_x(v):
            return place_x([v] + [shift_x(v, s) for s in range(1, nx)], 0)

        keep = (segment_ids % 2 == 1).astype(BF)
        masked = out_grad * keep[:, None]

        saved = lax.all_gather(jnp.stack([gate_pre, up_pre]), ("y", "x"), axis=0)

        pieces = jnp.broadcast_to(
            masked.reshape(nx, 1, part, width), (nx, nz, part, width)
        ).reshape(nx * nz * part, width)
        got = lax.all_to_all(pieces, ("x", "z"), 0, 0, tiled=True)
        got = got.reshape(nx, nz * part, width)

        down_own = gather_x(w_down)
        down_other = swap_core(down_own)

        def partial_hidden(weights):
            return jnp.einsum("xtd,xfd->tf", got, weights, preferred_element_type=F32).astype(BF)

        hidden_part = jnp.stack(
            [
                partial_hidden(down_own).reshape(ny, part, units),
                partial_hidden(down_other).reshape(ny, part, units),
            ],
            axis=1,
        )

        weights = gather_x(jnp.concatenate([tied(w_gate, got), w_up], axis=0))
        weights_other = swap_core(weights)

        rows = lax.all_gather(
            tied(jnp.concatenate([masked, inputs], axis=1), got), ("z", "core"), axis=0, tiled=True
        )

        terms = lax.all_to_all(
            hidden_part.reshape(ny * 2 * part, units), "y", 0, 0, tiled=True
        ).reshape(ny, 2 * part, units)
        hidden_sum = jnp.sum(terms.astype(F32), axis=0).astype(BF)
        copies = jnp.broadcast_to(hidden_sum[None], (ny, 2 * part, units))
        hidden_all = lax.all_to_all(
            copies.reshape(ny * 2 * part, units), "y", 0, 0, tiled=True
        ).reshape(ny, 2, part, units)
        hg_own, hg_other = hidden_all[:, 0], hidden_all[:, 1]

        saved = saved.reshape(ny, 2, nx // 2, 2, 2, part, units)
        gate_all = saved[:, :, :, 0].reshape(ny, 2, nx, part, units)
        up_all = saved[:, :, :, 1].reshape(ny, 2, nx, part, units)

        def pick(k):
            def one(a):
                return lax.dynamic_slice(a, (0, k, x, 0, 0), (ny, 1, 1, part, units)).reshape(
                    ny, part, units
                )

            return jnp.stack([one(gate_all), one(up_all)])

        saved_own = pick(core)
        saved_other = swap_core(pick(1 - core))

        def back(hidden_grad, gate_b, up_b):
            gate, up, grad = gate_b.astype(F32), up_b.astype(F32), hidden_grad.astype(F32)
            sig = jax.nn.sigmoid(gate)
            silu = gate * sig
            gate_grad = (grad * up * sig * (1.0 + gate * (1.0 - sig))).astype(BF)
            return gate_grad, (grad * silu).astype(BF), (silu * up).astype(BF)

        def partial_input(hg, pair, w):
            gate_grad, up_grad, _ = back(hg, pair[0], pair[1])
            w = w.reshape(nx, 2, width, units)
            grads = gate_grad.reshape(nz * part, units), up_grad.reshape(nz * part, units)
            return jnp.einsum(
                "tf,xdf->xtd", grads[0], w[:, 0], preferred_element_type=F32
            ) + jnp.einsum("tf,xdf->xtd", grads[1], w[:, 1], preferred_element_type=F32)

        input_part = (
            partial_input(hg_own, saved_own, weights)
            + partial_input(hg_other, saved_other, weights_other)
        ).astype(BF)
        input_terms = lax.all_to_all(
            input_part.reshape(nx * nz * part, width), ("x", "z"), 0, 0, tiled=True
        ).reshape(nx, nz, part, width)
        in_grad = jnp.sum(input_terms.astype(F32), axis=1).astype(BF).reshape(tokens, width)

        hg_here = jnp.zeros((ny, 2, part, units), BF)
        hg_here = lax.dynamic_update_slice_in_dim(hg_here, hg_own[:, None], core, 1)
        hg_here = lax.dynamic_update_slice_in_dim(
            hg_here, swap_core(hg_other)[:, None], 1 - core, 1
        )
        hg_all = place_x([hg_here] + [shift_x(hg_here, s) for s in range(1, nx)], 2)
        gate_grad, up_grad, hidden = (
            v.reshape(total, units) for v in back(hg_all, gate_all, up_all)
        )
        masked_rows, input_rows = rows[:, :width], rows[:, width:]

        def weight_grad(spec, a, b):
            return (jnp.einsum(spec, a, b, preferred_element_type=F32) * scale).astype(BF)

        grad_gate = weight_grad("td,tf->df", input_rows, gate_grad)
        grad_up = weight_grad("td,tf->df", input_rows, up_grad)
        grad_down = weight_grad("tf,td->fd", hidden, masked_rows)
        return in_grad, grad_gate, grad_up, grad_down

    return body


def solution(mesh):
    nx = 4 if mesh.shape["row"] >= 16 else 2
    ny, nz = mesh.shape["row"] // nx, mesh.shape["col"] // 2
    grid = Mesh(mesh.devices.reshape(ny, nx, nz, 2), ("y", "x", "z", "core"))
    row, col = ("y", "x"), ("z", "core")
    return jax.shard_map(
        make_body(ny, nx, nz),
        mesh=grid,
        in_specs=(
            P(col, row), P(col, row), P(row, col), P(row, col),
            P(row, col), P(row, col), P(col, row), P(col),
        ),
        out_specs=(P(col, row), P(row, col), P(row, col), P(col, row)),
        check_vma=False,
    )
```

```python
import functools
import jax
import jax.numpy as jnp
from jax import lax
from jax.experimental import pallas as pl
from jax.experimental.pallas import tpu as pltpu
from jax.sharding import Mesh, PartitionSpec as P

BF = jnp.bfloat16
F32 = jnp.float32
NT = (((1,), (1,)), ((), ()))
TN = (((0,), (0,)), ((), ()))


def tied(value, *others):
    return lax.optimization_barrier((value, *others))[0]


def back(hidden_grad, gate_b, up_b):
    gate, up, grad = gate_b.astype(F32), up_b.astype(F32), hidden_grad.astype(F32)
    sig = 1.0 / (1.0 + jnp.exp(-gate))
    silu = gate * sig
    gate_grad = (grad * up * sig * (1.0 + gate * (1.0 - sig))).astype(BF)
    return gate_grad, (grad * silu).astype(BF), (silu * up).astype(BF)


def hidden_kernel(nx, x_ref, got_ref, *refs):
    own, other, out_ref = refs[:nx], refs[nx : 2 * nx], refs[2 * nx]
    ny, two_part, units = out_ref.shape
    part = two_part // 2
    for half, blocks in enumerate((own, other)):
        total = None
        for s in range(nx):
            left = got_ref[lax.rem(x_ref[0] + nx - s, nx)]
            term = lax.dot_general(left, blocks[s][...], NT, preferred_element_type=F32)
            total = term if total is None else total + term
        out_ref[:, half * part : (half + 1) * part, :] = total.astype(BF).reshape(ny, part, units)


def input_kernel(hg_ref, own_ref, other_ref, w_own, w_other, out_ref, grads):
    nx, ny, two_part, units = hg_ref.shape
    part = two_part // 2
    total = None
    for half, (saved, w) in enumerate(((own_ref, w_own), (other_ref, w_other))):
        for x in range(nx):
            hg = hg_ref[x, :, half * part : (half + 1) * part, :].reshape(ny * part, units)
            both = saved[:, x // 2, x % 2].reshape(ny * part, 2 * units)
            gate_grad, up_grad, _ = back(hg, both[:, :units], both[:, units:])
            grads[half, :, x, :, :units] = gate_grad.reshape(ny, part, units)
            grads[half, :, x, :, units:] = up_grad.reshape(ny, part, units)
        left = grads[half].reshape(ny * nx * part, 2 * units)
        term = jnp.dot(left, w[...], preferred_element_type=F32)
        total = term if total is None else total + term
    out_ref[...] = total.astype(BF)


def down_kernel(scale, rows_ref, saved_ref, out_ref):
    units, width = out_ref.shape
    gate = saved_ref[:, :units].astype(F32)
    up = saved_ref[:, units:].astype(F32)
    hidden = (gate * (1.0 / (1.0 + jnp.exp(-gate))) * up).astype(BF)
    out = lax.dot_general(hidden, rows_ref[:, :width], TN, preferred_element_type=F32)
    out_ref[...] = (out * scale).astype(BF)


def weight_kernel(scale, place_ref, rows_ref, saved_ref, hg_ref, swapped_ref, *refs):
    gate_out, up_out, gate_all, up_all = refs
    nx, ny, two_part, units = hg_ref.shape
    part, width = two_part // 2, gate_out.shape[1]
    for half in range(2):
        core = place_ref[0] if half == 0 else 1 - place_ref[0]
        for x in range(nx):
            hg = hg_ref[x, :, :part, :] if half == 0 else swapped_ref[x]
            both = saved_ref[:, pl.ds(core, 1), x // 2, x % 2].reshape(ny * part, 2 * units)
            results = back(hg.reshape(ny * part, units), both[:, :units], both[:, units:])
            for ref, v in zip((gate_all, up_all), results):
                ref[:, pl.ds(core, 1), x] = v.reshape(ny, 1, part, units)
    inputs = rows_ref[:, width:]
    for out_ref, ref in ((gate_out, gate_all), (up_out, up_all)):
        left = ref[...].reshape(rows_ref.shape[0], units)
        out = lax.dot_general(left, inputs, TN, preferred_element_type=F32)
        out_ref[...] = (out * scale).astype(BF)


def call(kernel, out_shape, scratch, flops, *args):
    outs = [jax.ShapeDtypeStruct(shape, BF) for shape in out_shape]
    spaces = [pltpu.SMEM if a.dtype == jnp.int32 else pltpu.VMEM for a in args]
    return pl.pallas_call(
        kernel,
        out_shape=outs,
        in_specs=[pl.BlockSpec(memory_space=space) for space in spaces],
        out_specs=[pl.BlockSpec(memory_space=pltpu.VMEM)] * len(outs),
        scratch_shapes=[pltpu.VMEM(shape, BF) for shape in scratch],
        compiler_params=pltpu.CompilerParams(vmem_limit_bytes=48 * 1024 * 1024),
        cost_estimate=pl.CostEstimate(
            flops=flops, bytes_accessed=sum(a.size * 2 for a in args), transcendentals=0
        ),
    )(*args)


def make_body(ny, nx, nz):
    def shift_x(v, s):
        return lax.ppermute(v, "x", [(i, (i + s) % nx) for i in range(nx)])

    def swap_core(v):
        return lax.ppermute(v, "core", [(0, 1), (1, 0)])

    def body(inputs, out_grad, gate_pre, up_pre, w_gate, w_up, w_down, segment_ids):
        x, core = lax.axis_index("x"), lax.axis_index("core")
        place = jnp.stack([x]).astype(jnp.int32)
        tokens, width = inputs.shape
        units = w_down.shape[0]
        part = tokens // nx
        total = tokens * nz * 2
        scale = total ** (-0.5)

        down = [w_down] + [shift_x(w_down, s) for s in range(1, nx)]
        down_other = [swap_core(v) for v in down]
        both_w = jnp.concatenate([w_gate.T, w_up.T], axis=0)
        w_other = swap_core(both_w)

        saved = lax.all_gather(
            jnp.concatenate([gate_pre, up_pre], axis=1), ("y", "x"), axis=0
        ).reshape(ny, 2, nx // 2, 2, part, 2 * units)

        keep = (segment_ids % 2 == 1).astype(BF)
        masked = out_grad * keep[:, None]
        pieces = jnp.broadcast_to(
            (tied(out_grad) * keep[:, None]).reshape(nx, 1, part, width), (nx, nz, part, width)
        ).reshape(nx * nz * part, width)
        got = lax.all_to_all(pieces, ("x", "z"), 0, 0, tiled=True)
        got = got.reshape(nx, nz * part, width)

        (hidden_part,) = call(
            functools.partial(hidden_kernel, nx),
            [(ny, 2 * part, units)], [], 2 * total * units * width // 2,
            place, got, *down, *down_other,
        )
        rows = lax.all_gather(
            tied(jnp.concatenate([masked, inputs], axis=1), hidden_part),
            ("z", "core"), axis=0, tiled=True,
        )

        def spread(v, axis, count):
            shape = (count,) + v.shape
            copies = jnp.broadcast_to(v[None], shape).reshape((-1,) + v.shape[1:])
            return lax.all_to_all(copies, axis, 0, 0, tiled=True).reshape(shape)

        terms = lax.all_to_all(
            hidden_part.reshape(ny * 2 * part, units), "y", 0, 0, tiled=True
        ).reshape(ny, 2 * part, units)
        hidden_sum = jnp.sum(terms.astype(F32), axis=0).astype(BF)
        hidden_all = spread(spread(hidden_sum, "y", ny), "x", nx)
        swapped = swap_core(hidden_all[:, :, part:])

        def saved_at(k):
            return lax.dynamic_index_in_dim(saved, k, 1, keepdims=False)

        saved_other = swap_core(saved_at(1 - core))
        (input_part,) = call(
            input_kernel, [(nz * nx * part, width)], [(2, ny, nx, part, 2 * units)],
            2 * total * units * width,
            hidden_all, saved_at(core), saved_other, both_w, w_other,
        )
        input_terms = lax.all_to_all(tied(input_part, swapped), "z", 0, 0, tiled=True)

        (grad_down,) = call(
            functools.partial(down_kernel, scale),
            [(units, width)], [], 2 * total * units * width,
            rows, saved.reshape(total, 2 * units),
        )
        grad_gate, grad_up = call(
            functools.partial(weight_kernel, scale),
            [(units, width)] * 2, [(ny, 2, nx, part, units)] * 2, 4 * total * units * width,
            jnp.stack([core]).astype(jnp.int32), rows, saved, hidden_all, swapped,
        )

        input_terms = tied(input_terms, grad_gate, grad_up, grad_down)
        input_terms = input_terms.reshape(nz, tokens, width)
        in_grad = jnp.sum(input_terms.astype(F32), axis=0).astype(BF)
        return in_grad, grad_gate.T, grad_up.T, grad_down

    return body


def solution(mesh):
    nx = 4 if mesh.shape["row"] >= 16 else 2
    ny, nz = mesh.shape["row"] // nx, mesh.shape["col"] // 2
    grid = Mesh(mesh.devices.reshape(ny, nx, nz, 2), ("y", "x", "z", "core"))
    row, col = ("y", "x"), ("z", "core")
    return jax.shard_map(
        make_body(ny, nx, nz),
        mesh=grid,
        in_specs=(
            P(col, row), P(col, row), P(row, col), P(row, col),
            P(row, col), P(row, col), P(col, row), P(col),
        ),
        out_specs=(P(col, row), P(row, col), P(row, col), P(col, row)),
        check_vma=False,
    )
```

```python
import functools
import jax
import jax.numpy as jnp
from jax import lax
from jax.experimental import pallas as pl
from jax.experimental.pallas import tpu as pltpu
from jax.sharding import Mesh, PartitionSpec as P

BF = jnp.bfloat16
F32 = jnp.float32
NT = (((1,), (1,)), ((), ()))
TN = (((0,), (0,)), ((), ()))


def tied(value, *others):
    return lax.optimization_barrier((value, *others))[0]


def fetch(refs, bufs, sems):
    copies = [pltpu.make_async_copy(r, b, sems.at[i]) for i, (r, b) in enumerate(zip(refs, bufs))]
    for copy in copies:
        copy.start()
    return copies


def hidden_kernel(nx, x_ref, *refs):
    count = 2 * nx + 1
    sources, out_ref, bufs, sems = refs[:count], refs[-count - 2], refs[-count - 1 : -1], refs[-1]
    copies = fetch(sources, bufs, sems)
    ny, part, units = out_ref.shape[0], out_ref.shape[1], out_ref.shape[2] // 2
    copies[0].wait()
    for half in range(2):
        total = None
        for s in range(nx):
            i = 1 + half * nx + s
            copies[i].wait()
            left = bufs[0][lax.rem(x_ref[0] + nx - s, nx)]
            term = lax.dot_general(left, bufs[i][...], NT, preferred_element_type=F32)
            total = term if total is None else total + term
        total = total.astype(BF).reshape(ny, part, units)
        out_ref[:, :, half * units : (half + 1) * units] = total


def factor_kernel(core_ref, saved_ref, own_ref, send_ref, hidden_ref):
    ny, nx, part, units = own_ref.shape[1:]
    for half, ref in enumerate((own_ref, send_ref)):
        core = core_ref[0] if half == 0 else 1 - core_ref[0]

        for x in range(nx):
            both = saved_ref[:, pl.ds(core, 1), x].reshape(ny * part, 2 * units)
            gate, up = both[:, :units].astype(F32), both[:, units:].astype(F32)
            sig = 1.0 / (1.0 + jnp.exp(-gate))
            silu = gate * sig
            slope = (up * sig * (1.0 + gate * (1.0 - sig))).astype(BF)
            ref[0, :, x] = slope.reshape(ny, part, units)
            ref[1, :, x] = silu.astype(BF).reshape(ny, part, units)
            hidden = (silu * up).astype(BF).reshape(ny, 1, part, units)
            hidden_ref[:, pl.ds(core, 1), x] = hidden


def input_kernel(*refs):
    sources, (out_ref, send_ref, grads), bufs, sems = refs[:5], refs[6:9], refs[9:14], refs[14]
    copies = fetch(sources, bufs, sems)
    hg_ref = bufs[0]
    nx, ny, part, units = send_ref.shape
    copies[0].wait()
    total = None
    for half in range(2):
        factors, w = bufs[1 + 2 * half], bufs[2 + 2 * half]
        copies[1 + 2 * half].wait()

        for x in range(nx):
            hg = hg_ref[x, :, :, half * units : (half + 1) * units]
            if half == 1:
                send_ref[x] = hg
            grads[half, :, x, :, :units] = hg * factors[0, :, x]
            grads[half, :, x, :, units:] = hg * factors[1, :, x]
        copies[2 + 2 * half].wait()
        left = grads[half].reshape(ny * nx * part, 2 * units)
        term = jnp.dot(left, w[...], preferred_element_type=F32)
        total = term if total is None else total + term
    out_ref[...] = total.astype(BF)


def weight_kernel(scale, core_ref, rows_ref, hg_ref, swapped_ref, own_ref, send_ref, *refs):
    hidden_ref, gate_out, up_out, down_out, gate_all, up_all = refs
    nx, ny, part, units = swapped_ref.shape
    width = gate_out.shape[1]

    def dot(out_ref, a, b):
        out = lax.dot_general(
            a.reshape(rows_ref.shape[0], units), b, TN, preferred_element_type=F32
        )
        out_ref[...] = (out * scale).astype(BF)

    for half, factors in enumerate((own_ref, send_ref)):
        core = core_ref[0] if half == 0 else 1 - core_ref[0]

        for x in range(nx):
            hg = hg_ref[x, :, :, :units] if half == 0 else swapped_ref[x]
            gate_all[:, pl.ds(core, 1), x] = (hg * factors[0, :, x])[:, None]
            up_all[:, pl.ds(core, 1), x] = (hg * factors[1, :, x])[:, None]

    dot(down_out, hidden_ref[...], rows_ref[:, :width])
    dot(gate_out, gate_all[...], rows_ref[:, width:])
    dot(up_out, up_all[...], rows_ref[:, width:])


def mark_kernel(*refs):
    refs[-1][...] = jnp.zeros_like(refs[-1])


def order(us, *args):
    return pl.pallas_call(
        mark_kernel,
        out_shape=jax.ShapeDtypeStruct((16, 128), BF),
        in_specs=[pl.BlockSpec(memory_space=pl.ANY)] * len(args),
        cost_estimate=pl.CostEstimate(
            flops=us * 10**9, bytes_accessed=us * 3 * 10**6, transcendentals=0
        ),
    )(*args)


def call(kernel, out_shape, scratch, flops, *args, fetched=0):
    outs = [jax.ShapeDtypeStruct(shape, BF) for shape in out_shape]
    spaces = [pltpu.SMEM if a.dtype == jnp.int32 else pltpu.VMEM for a in args]
    scratches = [pltpu.VMEM(shape, BF) for shape in scratch]
    if fetched:
        spaces = [space if space == pltpu.SMEM else pl.ANY for space in spaces]
        big = [a for a in args if a.dtype != jnp.int32][:fetched]
        scratches += [pltpu.VMEM(a.shape, BF) for a in big] + [pltpu.SemaphoreType.DMA((fetched,))]
    return pl.pallas_call(
        kernel,
        out_shape=outs,
        in_specs=[pl.BlockSpec(memory_space=space) for space in spaces],
        out_specs=[pl.BlockSpec(memory_space=pltpu.VMEM)] * len(outs),
        scratch_shapes=scratches,
        compiler_params=pltpu.CompilerParams(vmem_limit_bytes=63 * 1024 * 1024),
        cost_estimate=pl.CostEstimate(
            flops=flops, bytes_accessed=sum(a.size * 2 for a in args), transcendentals=0
        ),
    )(*args)


def make_body(ny, nx, nz):
    def shift_x(v, s):
        return lax.ppermute(v, "x", [(i, (i + s) % nx) for i in range(nx)])

    def swap_core(v):
        return lax.ppermute(v, "core", [(0, 1), (1, 0)])

    def body(inputs, out_grad, gate_pre, up_pre, w_gate, w_up, w_down, segment_ids):
        x, core = lax.axis_index("x"), lax.axis_index("core")
        x_id, core_id = x.astype(jnp.int32).reshape(1), core.astype(jnp.int32).reshape(1)
        tokens, width = inputs.shape
        units = w_down.shape[0]
        part = tokens // nx
        total = tokens * nz * 2
        scale = total ** (-0.5)

        down = [w_down] + [shift_x(w_down, s) for s in range(1, nx)]
        down_other = [swap_core(v) for v in down]
        both_w = jnp.concatenate([w_gate.T, w_up.T], axis=0)
        w_other = swap_core(both_w)

        keep = (segment_ids % 2 == 1).astype(BF)
        masked = out_grad * keep[:, None]
        pieces = jnp.broadcast_to(
            masked.reshape(nx, 1, part, width), (nx, nz, part, width)
        ).reshape(nx * nz * part, width)
        saved = lax.all_gather(
            tied(jnp.concatenate([gate_pre, up_pre], axis=1), pieces), ("y", "x"), axis=0
        ).reshape(ny, 2, nx, part, 2 * units)
        got = lax.all_to_all(pieces, ("x", "z"), 0, 0, tiled=True)
        got = got.reshape(nx, nz * part, width)

        mark = order(20, *down[1:])
        (hidden_part,) = call(
            functools.partial(hidden_kernel, nx),
            [(ny, part, 2 * units)], [], 2 * total * units * width // 2,
            x_id, got, *down, *down_other, mark, fetched=2 * nx + 1,
        )
        rows = lax.all_gather(
            tied(jnp.concatenate([masked, inputs], axis=1), hidden_part),
            ("z", "core"), axis=0, tiled=True,
        )

        def spread(v, axis, count):
            shape = (count,) + v.shape
            copies = jnp.broadcast_to(v[None], shape).reshape((-1,) + v.shape[1:])
            return lax.all_to_all(copies, axis, 0, 0, tiled=True).reshape(shape)

        terms = lax.all_to_all(
            hidden_part.reshape(ny * part, 2 * units), "y", 0, 0, tiled=True
        ).reshape(ny, part, 2 * units)
        hidden_sum = jnp.sum(terms.astype(F32), axis=0).astype(BF)
        hidden_y = spread(hidden_sum, "y", ny)
        hidden_all = spread(hidden_y, "x", nx)

        pair = (2, ny, nx, part, units)
        factors, factors_send, hidden = call(
            factor_kernel, [pair, pair, (ny, 2, nx, part, units)], [],
            15000 * total * units, core_id, tied(saved, hidden_y),
        )
        factors_other = swap_core(factors_send)
        input_part, hg_send = call(
            input_kernel, [(nz * nx * part, width), (nx, ny, part, units)],
            [(2, ny, nx, part, 2 * units)], 2 * total * units * width,
            hidden_all, factors, both_w, factors_other, w_other, order(60, hidden_all), fetched=5,
        )
        swapped = swap_core(hg_send)
        input_terms = lax.all_to_all(input_part, "z", 0, 0, tiled=True)
        grad_gate, grad_up, grad_down = call(
            functools.partial(weight_kernel, scale),
            [(units, width)] * 3, [(ny, 2, nx, part, units)] * 2, 200 * total * units * width,
            core_id, rows, hidden_all, swapped, factors, factors_send, hidden,
        )

        input_terms = tied(input_terms, grad_gate, grad_up, grad_down)
        input_terms = input_terms.reshape(nz, tokens, width)
        in_grad = jnp.sum(input_terms.astype(F32), axis=0).astype(BF)
        return in_grad, grad_gate.T, grad_up.T, grad_down

    return body


def solution(mesh):
    nx = 4 if mesh.shape["row"] >= 16 else 2
    ny, nz = mesh.shape["row"] // nx, mesh.shape["col"] // 2
    grid = Mesh(mesh.devices.reshape(ny, nx, nz, 2), ("y", "x", "z", "core"))
    row, col = ("y", "x"), ("z", "core")
    return jax.shard_map(
        make_body(ny, nx, nz),
        mesh=grid,
        in_specs=(
            P(col, row), P(col, row), P(row, col), P(row, col),
            P(row, col), P(row, col), P(col, row), P(col),
        ),
        out_specs=(P(col, row), P(row, col), P(row, col), P(col, row)),
        check_vma=False,
    )
```

```python
import functools
import jax
import jax.numpy as jnp
from jax import lax
from jax.experimental import pallas as pl
from jax.experimental.pallas import tpu as pltpu
from jax.sharding import Mesh, PartitionSpec as P

BF = jnp.bfloat16
F32 = jnp.float32
NT = (((1,), (1,)), ((), ()))
TN = (((0,), (0,)), ((), ()))


def tied(value, *others):
    return lax.optimization_barrier((value, *others))[0]


def fetch(refs, bufs, sems):
    copies = [pltpu.make_async_copy(r, b, sems.at[i]) for i, (r, b) in enumerate(zip(refs, bufs))]
    for copy in copies:
        copy.start()
    return copies


def hidden_kernel(nx, x_ref, *refs):
    count = 2 * nx + 1
    sources, out_ref, bufs, sems = refs[:count], refs[-count - 2], refs[-count - 1 : -1], refs[-1]
    copies = fetch(sources, bufs, sems)
    ny, part, units = out_ref.shape[0], out_ref.shape[1], out_ref.shape[2] // 2
    copies[0].wait()
    for half in range(2):
        total = None
        for s in range(nx):
            i = 1 + half * nx + s
            copies[i].wait()
            left = bufs[0][lax.rem(x_ref[0] + nx - s, nx)]
            term = lax.dot_general(left, bufs[i][...], NT, preferred_element_type=F32)
            total = term if total is None else total + term
        total = total.astype(BF).reshape(ny, part, units)
        out_ref[:, :, half * units : (half + 1) * units] = total


def factor_kernel(core_ref, saved_ref, own_ref, send_ref, hidden_ref):
    ny, nx, part, units = own_ref.shape[1:]
    for half, ref in enumerate((own_ref, send_ref)):
        core = core_ref[0] if half == 0 else 1 - core_ref[0]

        for x in range(nx):
            both = saved_ref[:, pl.ds(core, 1), x].reshape(ny * part, 2 * units)
            gate, up = both[:, :units].astype(F32), both[:, units:].astype(F32)
            sig = 1.0 / (1.0 + jnp.exp(-gate))
            silu = gate * sig
            slope = (up * sig * (1.0 + gate * (1.0 - sig))).astype(BF)
            ref[0, :, x] = slope.reshape(ny, part, units)
            ref[1, :, x] = silu.astype(BF).reshape(ny, part, units)
            hidden = (silu * up).astype(BF).reshape(ny, 1, part, units)
            hidden_ref[:, pl.ds(core, 1), x] = hidden


def input_kernel(*refs):
    sources, (out_ref, send_ref, grads), bufs, sems = refs[:5], refs[6:9], refs[9:14], refs[14]
    copies = fetch(sources, bufs, sems)
    hg_ref = bufs[0]
    nx, ny, part, units = send_ref.shape
    copies[0].wait()
    total = None
    for half in range(2):
        factors, w = bufs[1 + 2 * half], bufs[2 + 2 * half]
        copies[1 + 2 * half].wait()

        for x in range(nx):
            hg = hg_ref[x, :, :, half * units : (half + 1) * units]
            if half == 1:
                send_ref[x] = hg
            grads[half, :, x, :, :units] = hg * factors[0, :, x]
            grads[half, :, x, :, units:] = hg * factors[1, :, x]
        copies[2 + 2 * half].wait()
        left = grads[half].reshape(ny * nx * part, 2 * units)
        term = jnp.dot(left, w[...], preferred_element_type=F32)
        total = term if total is None else total + term
    out_ref[...] = total.astype(BF)


def weight_kernel(scale, core_ref, rows_ref, hg_ref, swapped_ref, own_ref, send_ref, *refs):
    hidden_ref, gate_out, up_out, down_out, gate_all, up_all = refs
    nx, ny, part, units = swapped_ref.shape
    width = gate_out.shape[1]

    def dot(out_ref, a, b):
        out = lax.dot_general(
            a.reshape(rows_ref.shape[0], units), b, TN, preferred_element_type=F32
        )
        out_ref[...] = (out * scale).astype(BF)

    for half, factors in enumerate((own_ref, send_ref)):
        core = core_ref[0] if half == 0 else 1 - core_ref[0]

        for x in range(nx):
            hg = hg_ref[x, :, :, :units] if half == 0 else swapped_ref[x]
            gate_all[:, pl.ds(core, 1), x] = (hg * factors[0, :, x])[:, None]
            up_all[:, pl.ds(core, 1), x] = (hg * factors[1, :, x])[:, None]

    dot(down_out, hidden_ref[...], rows_ref[:, :width])
    dot(gate_out, gate_all[...], rows_ref[:, width:])
    dot(up_out, up_all[...], rows_ref[:, width:])


def mark_kernel(*refs):
    refs[-1][...] = jnp.zeros_like(refs[-1])


def order(us, *args):
    return pl.pallas_call(
        mark_kernel,
        out_shape=jax.ShapeDtypeStruct((16, 128), BF),
        in_specs=[pl.BlockSpec(memory_space=pl.ANY)] * len(args),
        cost_estimate=pl.CostEstimate(
            flops=us * 10**9, bytes_accessed=us * 3 * 10**6, transcendentals=0
        ),
    )(*args)


def call(kernel, out_shape, scratch, flops, *args, fetched=0):
    outs = [jax.ShapeDtypeStruct(shape, BF) for shape in out_shape]
    spaces = [pltpu.SMEM if a.dtype == jnp.int32 else pltpu.VMEM for a in args]
    scratches = [pltpu.VMEM(shape, BF) for shape in scratch]
    if fetched:
        spaces = [space if space == pltpu.SMEM else pl.ANY for space in spaces]
        big = [a for a in args if a.dtype != jnp.int32][:fetched]
        scratches += [pltpu.VMEM(a.shape, BF) for a in big] + [pltpu.SemaphoreType.DMA((fetched,))]
    return pl.pallas_call(
        kernel,
        out_shape=outs,
        in_specs=[pl.BlockSpec(memory_space=space) for space in spaces],
        out_specs=[pl.BlockSpec(memory_space=pltpu.VMEM)] * len(outs),
        scratch_shapes=scratches,
        compiler_params=pltpu.CompilerParams(vmem_limit_bytes=63 * 1024 * 1024),
        cost_estimate=pl.CostEstimate(
            flops=flops, bytes_accessed=sum(a.size * 2 for a in args), transcendentals=0
        ),
    )(*args)


def make_body(ny, nx, nz):
    def shift_x(v, s):
        return lax.ppermute(v, "x", [(i, (i + s) % nx) for i in range(nx)])

    def swap_core(v):
        return lax.ppermute(v, "core", [(0, 1), (1, 0)])

    def body(inputs, out_grad, gate_pre, up_pre, w_gate, w_up, w_down, segment_ids):
        x, core = lax.axis_index("x"), lax.axis_index("core")
        x_id, core_id = x.astype(jnp.int32).reshape(1), core.astype(jnp.int32).reshape(1)
        tokens, width = inputs.shape
        units = w_down.shape[0]
        part = tokens // nx
        total = tokens * nz * 2
        scale = total ** (-0.5)

        down = [w_down] + [shift_x(w_down, s) for s in range(1, nx)]
        down_other = [swap_core(v) for v in down]
        both_w = jnp.concatenate([w_gate.T, w_up.T], axis=0)
        w_other = swap_core(both_w)

        keep = (segment_ids % 2 == 1).astype(BF)
        masked = out_grad * keep[:, None]
        pieces = jnp.broadcast_to(
            masked.reshape(nx, 1, part, width), (nx, nz, part, width)
        ).reshape(nx * nz * part, width)
        saved = lax.all_gather(
            tied(jnp.concatenate([gate_pre, up_pre], axis=1), pieces), ("y", "x"), axis=0
        ).reshape(ny, 2, nx, part, 2 * units)
        got = lax.all_to_all(pieces, ("x", "z"), 0, 0, tiled=True)
        got = got.reshape(nx, nz * part, width)

        mark = order(20, *down[1:])
        (hidden_part,) = call(
            functools.partial(hidden_kernel, nx),
            [(ny, part, 2 * units)], [], 2 * total * units * width // 2,
            x_id, got, *down, *down_other, mark, w_other, fetched=2 * nx + 1,
        )
        rows = lax.all_gather(
            jnp.concatenate([tied(out_grad, hidden_part) * keep[:, None], inputs], axis=1),
            ("z", "core"), axis=0, tiled=True,
        )

        def spread(v, axis, count):
            shape = (count,) + v.shape
            copies = jnp.broadcast_to(v[None], shape).reshape((-1,) + v.shape[1:])
            return lax.all_to_all(copies, axis, 0, 0, tiled=True).reshape(shape)

        terms = lax.all_to_all(
            hidden_part.reshape(ny * part, 2 * units), "y", 0, 0, tiled=True
        ).reshape(ny, part, 2 * units)
        hidden_sum = jnp.sum(terms.astype(F32), axis=0).astype(BF)
        hidden_y = spread(hidden_sum, "y", ny)
        hidden_all = spread(hidden_y, "x", nx)

        pair = (2, ny, nx, part, units)
        factors, factors_send, hidden = call(
            factor_kernel, [pair, pair, (ny, 2, nx, part, units)], [],
            15000 * total * units, core_id, tied(saved, hidden_y),
        )
        factors_other = swap_core(factors_send)
        input_part, hg_send = call(
            input_kernel, [(nz * nx * part, width), (nx, ny, part, units)],
            [(2, ny, nx, part, 2 * units)], 2 * total * units * width,
            hidden_all, factors, both_w, factors_other, w_other, order(60, hidden_all), fetched=5,
        )
        swapped = swap_core(hg_send)
        input_terms = lax.all_to_all(input_part, "z", 0, 0, tiled=True)
        grad_gate, grad_up, grad_down = call(
            functools.partial(weight_kernel, scale),
            [(units, width)] * 3, [(ny, 2, nx, part, units)] * 2, 200 * total * units * width,
            core_id, rows, hidden_all, swapped, factors, factors_send, hidden,
        )

        input_terms = tied(input_terms, grad_gate, grad_up, grad_down)
        input_terms = input_terms.reshape(nz, tokens, width)
        in_grad = jnp.sum(input_terms.astype(F32), axis=0).astype(BF)
        return in_grad, grad_gate.T, grad_up.T, grad_down

    return body


def solution(mesh):
    nx = 4 if mesh.shape["row"] >= 16 else 2
    ny, nz = mesh.shape["row"] // nx, mesh.shape["col"] // 2
    grid = Mesh(mesh.devices.reshape(ny, nx, nz, 2), ("y", "x", "z", "core"))
    row, col = ("y", "x"), ("z", "core")
    return jax.shard_map(
        make_body(ny, nx, nz),
        mesh=grid,
        in_specs=(
            P(col, row), P(col, row), P(row, col), P(row, col),
            P(row, col), P(row, col), P(col, row), P(col),
        ),
        out_specs=(P(col, row), P(row, col), P(row, col), P(col, row)),
        check_vma=False,
    )
```

```python
import functools
import jax
import jax.numpy as jnp
from jax import lax
from jax.experimental import pallas as pl
from jax.experimental.pallas import tpu as pltpu
from jax.sharding import Mesh, PartitionSpec as P

BF = jnp.bfloat16
F32 = jnp.float32
NT = (((1,), (1,)), ((), ()))
TN = (((0,), (0,)), ((), ()))


def tied(value, *others):
    return lax.optimization_barrier((value, *others))[0]


def fetch(refs, bufs, sems):
    copies = [pltpu.make_async_copy(r, b, sems.at[i]) for i, (r, b) in enumerate(zip(refs, bufs))]
    for copy in copies:
        copy.start()
    return copies


def hidden_kernel(nx, x_ref, *refs):
    count = 2 * nx + 1
    sources, out_ref, bufs, sems = refs[:count], refs[-count - 2], refs[-count - 1 : -1], refs[-1]
    copies = fetch(sources, bufs, sems)
    ny, part, units = out_ref.shape[0], out_ref.shape[1], out_ref.shape[2] // 2
    copies[0].wait()
    for half in range(2):
        total = None
        for s in range(nx):
            i = 1 + half * nx + s
            copies[i].wait()
            left = bufs[0][lax.rem(x_ref[0] + nx - s, nx)]
            term = lax.dot_general(left, bufs[i][...], NT, preferred_element_type=F32)
            total = term if total is None else total + term
        total = total.astype(BF).reshape(ny, part, units)
        out_ref[:, :, half * units : (half + 1) * units] = total


def factor_kernel(core_ref, saved_ref, own_ref, send_ref, hidden_ref):
    ny, nx, part, units = own_ref.shape[1:]
    for half, ref in enumerate((own_ref, send_ref)):
        core = core_ref[0] if half == 0 else 1 - core_ref[0]

        for x in range(nx):
            both = saved_ref[:, pl.ds(core, 1), x].reshape(ny * part, 2 * units)
            gate, up = both[:, :units].astype(F32), both[:, units:].astype(F32)
            sig = 1.0 / (1.0 + jnp.exp(-gate))
            silu = gate * sig
            slope = (up * sig * (1.0 + gate * (1.0 - sig))).astype(BF)
            ref[0, :, x] = slope.reshape(ny, part, units)
            ref[1, :, x] = silu.astype(BF).reshape(ny, part, units)
            hidden = (silu * up).astype(BF).reshape(ny, 1, part, units)
            hidden_ref[:, pl.ds(core, 1), x] = hidden


def input_kernel(*refs):
    sources, (out_ref, send_ref, grads), bufs, sems = refs[:5], refs[6:9], refs[9:14], refs[14]
    copies = fetch(sources, bufs, sems)
    hg_ref = bufs[0]
    nx, ny, part, units = send_ref.shape
    copies[0].wait()
    total = None
    for half in range(2):
        factors, w = bufs[1 + 2 * half], bufs[2 + 2 * half]
        copies[1 + 2 * half].wait()

        for x in range(nx):
            hg = hg_ref[x, :, :, half * units : (half + 1) * units]
            if half == 1:
                send_ref[x] = hg
            grads[half, :, x, :, :units] = hg * factors[0, :, x]
            grads[half, :, x, :, units:] = hg * factors[1, :, x]
        copies[2 + 2 * half].wait()
        left = grads[half].reshape(ny * nx * part, 2 * units)
        term = jnp.dot(left, w[...], preferred_element_type=F32)
        total = term if total is None else total + term
    out_ref[...] = total.astype(BF)


def weight_kernel(scale, core_ref, rows_ref, hg_ref, swapped_ref, own_ref, send_ref, *refs):
    hidden_ref, gate_out, up_out, down_out, gate_all, up_all = refs
    nx, ny, part, units = swapped_ref.shape
    width = gate_out.shape[1]

    def dot(out_ref, a, b):
        out = lax.dot_general(
            a.reshape(rows_ref.shape[0], units), b, TN, preferred_element_type=F32
        )
        out_ref[...] = (out * scale).astype(BF)

    for half, factors in enumerate((own_ref, send_ref)):
        core = core_ref[0] if half == 0 else 1 - core_ref[0]

        for x in range(nx):
            hg = hg_ref[x, :, :, :units] if half == 0 else swapped_ref[x]
            gate_all[:, pl.ds(core, 1), x] = (hg * factors[0, :, x])[:, None]
            up_all[:, pl.ds(core, 1), x] = (hg * factors[1, :, x])[:, None]

    dot(down_out, hidden_ref[...], rows_ref[:, :width])
    dot(gate_out, gate_all[...], rows_ref[:, width:])
    dot(up_out, up_all[...], rows_ref[:, width:])


def mark_kernel(*refs):
    refs[-1][...] = jnp.zeros_like(refs[-1])


def order(us, *args):
    return pl.pallas_call(
        mark_kernel,
        out_shape=jax.ShapeDtypeStruct((16, 128), BF),
        in_specs=[pl.BlockSpec(memory_space=pl.ANY)] * len(args),
        cost_estimate=pl.CostEstimate(
            flops=us * 10**9, bytes_accessed=us * 3 * 10**6, transcendentals=0
        ),
    )(*args)


def call(kernel, out_shape, scratch, flops, *args, fetched=0, mib=63):
    outs = [jax.ShapeDtypeStruct(shape, BF) for shape in out_shape]
    spaces = [pltpu.SMEM if a.dtype == jnp.int32 else pltpu.VMEM for a in args]
    scratches = [pltpu.VMEM(shape, BF) for shape in scratch]
    if fetched:
        spaces = [space if space == pltpu.SMEM else pl.ANY for space in spaces]
        big = [a for a in args if a.dtype != jnp.int32][:fetched]
        scratches += [pltpu.VMEM(a.shape, BF) for a in big] + [pltpu.SemaphoreType.DMA((fetched,))]
    return pl.pallas_call(
        kernel,
        out_shape=outs,
        in_specs=[pl.BlockSpec(memory_space=space) for space in spaces],
        out_specs=[pl.BlockSpec(memory_space=pltpu.VMEM)] * len(outs),
        scratch_shapes=scratches,
        compiler_params=pltpu.CompilerParams(vmem_limit_bytes=mib * 1024 * 1024),
        cost_estimate=pl.CostEstimate(
            flops=flops, bytes_accessed=sum(a.size * 2 for a in args), transcendentals=0
        ),
    )(*args)


def make_body(ny, nx, nz):
    def shift_x(v, s):
        return lax.ppermute(v, "x", [(i, (i + s) % nx) for i in range(nx)])

    def swap_core(v):
        return lax.ppermute(v, "core", [(0, 1), (1, 0)])

    def body(inputs, out_grad, gate_pre, up_pre, w_gate, w_up, w_down, segment_ids):
        x, core = lax.axis_index("x"), lax.axis_index("core")
        x_id, core_id = x.astype(jnp.int32).reshape(1), core.astype(jnp.int32).reshape(1)
        tokens, width = inputs.shape
        units = w_down.shape[0]
        part = tokens // nx
        total = tokens * nz * 2
        scale = total ** (-0.5)

        down = [w_down] + [shift_x(w_down, s) for s in range(1, nx)]
        down_other = [swap_core(v) for v in down]
        both_w = jnp.concatenate([w_gate.T, w_up.T], axis=0)
        w_other = swap_core(both_w)

        keep = (segment_ids % 2 == 1).astype(BF)
        masked = out_grad * keep[:, None]
        pieces = jnp.broadcast_to(
            masked.reshape(nx, 1, part, width), (nx, nz, part, width)
        ).reshape(nx * nz * part, width)
        saved = lax.all_gather(
            tied(jnp.concatenate([gate_pre, up_pre], axis=1), pieces), ("y", "x"), axis=0
        ).reshape(ny, 2, nx, part, 2 * units)
        got = lax.all_to_all(pieces, ("x", "z"), 0, 0, tiled=True)
        got = got.reshape(nx, nz * part, width)

        mark = order(20, *down[1:])
        (hidden_part,) = call(
            functools.partial(hidden_kernel, nx),
            [(ny, part, 2 * units)], [], 2 * total * units * width // 2,
            x_id, got, *down, *down_other, mark, w_other, fetched=2 * nx + 1,
        )
        rows = lax.all_gather(
            jnp.concatenate([tied(out_grad, hidden_part) * keep[:, None], inputs], axis=1),
            ("z", "core"), axis=0, tiled=True,
        )

        def spread(v, axis, count):
            shape = (count,) + v.shape
            copies = jnp.broadcast_to(v[None], shape).reshape((-1,) + v.shape[1:])
            return lax.all_to_all(copies, axis, 0, 0, tiled=True).reshape(shape)

        terms = lax.all_to_all(
            hidden_part.reshape(ny * part, 2 * units), "y", 0, 0, tiled=True
        ).reshape(ny, part, 2 * units)
        hidden_sum = jnp.sum(terms.astype(F32), axis=0).astype(BF)
        hidden_y = spread(hidden_sum, "y", ny)
        hidden_all = spread(hidden_y, "x", nx)

        pair = (2, ny, nx, part, units)
        factors, factors_send, hidden = call(
            factor_kernel, [pair, pair, (ny, 2, nx, part, units)], [],
            15000 * total * units, core_id, tied(saved, hidden_y),
        )
        factors_other = swap_core(factors_send)
        input_part, hg_send = call(
            input_kernel, [(nz * nx * part, width), (nx, ny, part, units)],
            [(2, ny, nx, part, 2 * units)], 2 * total * units * width,
            hidden_all, factors, both_w, factors_other, w_other, order(60, hidden_all), fetched=5,
        )
        swapped = swap_core(hg_send)
        input_terms = lax.all_to_all(input_part, "z", 0, 0, tiled=True)
        grad_gate, grad_up, grad_down = call(
            functools.partial(weight_kernel, scale),
            [(units, width)] * 3, [(ny, 2, nx, part, units)] * 2, 200 * total * units * width,
            core_id, rows, hidden_all, swapped, factors, factors_send, hidden, mib=62,
        )

        input_terms = tied(input_terms, grad_gate, grad_up, grad_down)
        input_terms = input_terms.reshape(nz, tokens, width)
        in_grad = jnp.sum(input_terms.astype(F32), axis=0).astype(BF)
        return in_grad, grad_gate.T, grad_up.T, grad_down

    return body


def solution(mesh):
    nx = 4 if mesh.shape["row"] >= 16 else 2
    ny, nz = mesh.shape["row"] // nx, mesh.shape["col"] // 2
    grid = Mesh(mesh.devices.reshape(ny, nx, nz, 2), ("y", "x", "z", "core"))
    row, col = ("y", "x"), ("z", "core")
    return jax.shard_map(
        make_body(ny, nx, nz),
        mesh=grid,
        in_specs=(
            P(col, row), P(col, row), P(row, col), P(row, col),
            P(row, col), P(row, col), P(col, row), P(col),
        ),
        out_specs=(P(col, row), P(row, col), P(row, col), P(col, row)),
        check_vma=False,
    )
```

```python
import functools
import jax
import jax.numpy as jnp
from jax import lax
from jax.experimental import pallas as pl
from jax.experimental.pallas import tpu as pltpu
from jax.sharding import Mesh, PartitionSpec as P

BF = jnp.bfloat16
F32 = jnp.float32
NT = (((1,), (1,)), ((), ()))
TN = (((0,), (0,)), ((), ()))


def tied(value, *others):
    return lax.optimization_barrier((value, *others))[0]


def fetch(refs, bufs, sems):
    copies = [pltpu.make_async_copy(r, b, sems.at[i]) for i, (r, b) in enumerate(zip(refs, bufs))]
    for copy in copies:
        copy.start()
    return copies


def hidden_kernel(nx, x_ref, *refs):
    count = 2 * nx + 1
    sources, out_ref, bufs, sems = refs[:count], refs[-count - 2], refs[-count - 1 : -1], refs[-1]
    copies = fetch(sources, bufs, sems)
    ny, part, units = out_ref.shape[0], out_ref.shape[1], out_ref.shape[2] // 2
    copies[0].wait()
    for half in range(2):
        total = None
        for s in range(nx):
            i = 1 + half * nx + s
            copies[i].wait()
            left = bufs[0][lax.rem(x_ref[0] + nx - s, nx)]
            term = lax.dot_general(left, bufs[i][...], NT, preferred_element_type=F32)
            total = term if total is None else total + term
        total = total.astype(BF).reshape(ny, part, units)
        out_ref[:, :, half * units : (half + 1) * units] = total


def piece_kernel(grad_ref, keep_ref, out_ref):
    nx, nz, part, _ = out_ref.shape
    for x in range(nx):
        cut = slice(x * part, (x + 1) * part)
        block = grad_ref[cut, :] * keep_ref[cut, :]
        for z in range(nz):
            out_ref[x, z] = block


def sum_kernel(terms_ref, out_ref):
    total = jnp.sum(terms_ref[...].astype(F32), axis=0).astype(BF)
    for y in range(out_ref.shape[0]):
        out_ref[y] = total


def factor_kernel(core_ref, saved_ref, own_ref, send_ref, hidden_ref):
    ny, nx, part, units = own_ref.shape[1:]
    for half, ref in enumerate((own_ref, send_ref)):
        core = core_ref[0] if half == 0 else 1 - core_ref[0]

        for x in range(nx):
            both = saved_ref[:, pl.ds(core, 1), x].reshape(ny * part, 2 * units)
            gate, up = both[:, :units].astype(F32), both[:, units:].astype(F32)
            sig = 1.0 / (1.0 + jnp.exp(-gate))
            silu = gate * sig
            slope = (up * sig * (1.0 + gate * (1.0 - sig))).astype(BF)
            ref[0, :, x] = slope.reshape(ny, part, units)
            ref[1, :, x] = silu.astype(BF).reshape(ny, part, units)
            hidden = (silu * up).astype(BF).reshape(ny, 1, part, units)
            hidden_ref[:, pl.ds(core, 1), x] = hidden


def input_kernel(*refs):
    sources, (out_ref, send_ref, grads), bufs, sems = refs[:5], refs[6:9], refs[9:14], refs[14]
    copies = fetch(sources, bufs, sems)
    hg_ref = bufs[0]
    nx, ny, part, units = send_ref.shape
    copies[0].wait()
    total = None
    for half in range(2):
        factors, w = bufs[1 + 2 * half], bufs[2 + 2 * half]
        copies[1 + 2 * half].wait()

        for x in range(nx):
            hg = hg_ref[x, :, :, half * units : (half + 1) * units]
            if half == 1:
                send_ref[x] = hg
            grads[half, :, x, :, :units] = hg * factors[0, :, x]
            grads[half, :, x, :, units:] = hg * factors[1, :, x]
        copies[2 + 2 * half].wait()
        left = grads[half].reshape(ny * nx * part, 2 * units)
        term = jnp.dot(left, w[...], preferred_element_type=F32)
        total = term if total is None else total + term
    out_ref[...] = total.astype(BF)


def weight_kernel(scale, core_ref, rows_ref, hg_ref, swapped_ref, own_ref, send_ref, *refs):
    hidden_ref, gate_out, up_out, down_out, gate_all, up_all = refs
    nx, ny, part, units = swapped_ref.shape
    width = gate_out.shape[1]

    def dot(out_ref, a, b):
        out = lax.dot_general(
            a.reshape(rows_ref.shape[0], units), b, TN, preferred_element_type=F32
        )
        out_ref[...] = (out * scale).astype(BF)

    for half, factors in enumerate((own_ref, send_ref)):
        core = core_ref[0] if half == 0 else 1 - core_ref[0]

        for x in range(nx):
            hg = hg_ref[x, :, :, :units] if half == 0 else swapped_ref[x]
            gate_all[:, pl.ds(core, 1), x] = (hg * factors[0, :, x])[:, None]
            up_all[:, pl.ds(core, 1), x] = (hg * factors[1, :, x])[:, None]

    dot(down_out, hidden_ref[...], rows_ref[:, :width])
    dot(gate_out, gate_all[...], rows_ref[:, width:])
    dot(up_out, up_all[...], rows_ref[:, width:])


def mark_kernel(*refs):
    refs[-1][...] = jnp.zeros_like(refs[-1])


def order(us, *args):
    return pl.pallas_call(
        mark_kernel,
        out_shape=jax.ShapeDtypeStruct((16, 128), BF),
        in_specs=[pl.BlockSpec(memory_space=pl.ANY)] * len(args),
        cost_estimate=pl.CostEstimate(
            flops=us * 10**9, bytes_accessed=us * 3 * 10**6, transcendentals=0
        ),
    )(*args)


def call(kernel, out_shape, scratch, flops, *args, fetched=0, mib=63):
    outs = [jax.ShapeDtypeStruct(shape, BF) for shape in out_shape]
    spaces = [pltpu.SMEM if a.dtype == jnp.int32 else pltpu.VMEM for a in args]
    scratches = [pltpu.VMEM(shape, BF) for shape in scratch]
    if fetched:
        spaces = [space if space == pltpu.SMEM else pl.ANY for space in spaces]
        big = [a for a in args if a.dtype != jnp.int32][:fetched]
        scratches += [pltpu.VMEM(a.shape, BF) for a in big] + [pltpu.SemaphoreType.DMA((fetched,))]
    return pl.pallas_call(
        kernel,
        out_shape=outs,
        in_specs=[pl.BlockSpec(memory_space=space) for space in spaces],
        out_specs=[pl.BlockSpec(memory_space=pltpu.VMEM)] * len(outs),
        scratch_shapes=scratches,
        compiler_params=pltpu.CompilerParams(vmem_limit_bytes=mib * 1024 * 1024),
        cost_estimate=pl.CostEstimate(
            flops=flops, bytes_accessed=sum(a.size * 2 for a in args), transcendentals=0
        ),
    )(*args)


def make_body(ny, nx, nz):
    def shift_x(v, s):
        return lax.ppermute(v, "x", [(i, (i + s) % nx) for i in range(nx)])

    def swap_core(v):
        return lax.ppermute(v, "core", [(0, 1), (1, 0)])

    def body(inputs, out_grad, gate_pre, up_pre, w_gate, w_up, w_down, segment_ids):
        x, core = lax.axis_index("x"), lax.axis_index("core")
        x_id, core_id = x.astype(jnp.int32).reshape(1), core.astype(jnp.int32).reshape(1)
        tokens, width = inputs.shape
        units = w_down.shape[0]
        part = tokens // nx
        total = tokens * nz * 2
        scale = total ** (-0.5)

        down = [w_down] + [shift_x(w_down, s) for s in range(1, nx)]
        down_other = [swap_core(v) for v in down]
        both_w = jnp.concatenate([w_gate.T, w_up.T], axis=0)
        w_other = swap_core(both_w)

        keep = (segment_ids % 2 == 1).astype(BF)
        (pieces,) = call(
            piece_kernel, [(nx, nz, part, width)], [], 10**6, out_grad, keep[:, None], mib=16
        )
        pieces = pieces.reshape(nx * nz * part, width)
        saved = lax.all_gather(
            tied(jnp.concatenate([gate_pre, up_pre], axis=1), pieces), ("y", "x"), axis=0
        ).reshape(ny, 2, nx, part, 2 * units)
        got = lax.all_to_all(pieces, ("x", "z"), 0, 0, tiled=True)
        got = got.reshape(nx, nz * part, width)

        mark = order(20, *down[1:])
        (hidden_part,) = call(
            functools.partial(hidden_kernel, nx),
            [(ny, part, 2 * units)], [], 2 * total * units * width // 2,
            x_id, got, *down, *down_other, mark, w_other, fetched=2 * nx + 1,
        )
        rows = lax.all_gather(
            jnp.concatenate([tied(out_grad, hidden_part) * keep[:, None], inputs], axis=1),
            ("z", "core"), axis=0, tiled=True,
        )

        def spread(v, axis, count):
            shape = (count,) + v.shape
            copies = jnp.broadcast_to(v[None], shape).reshape((-1,) + v.shape[1:])
            return lax.all_to_all(copies, axis, 0, 0, tiled=True).reshape(shape)

        terms = lax.all_to_all(
            hidden_part.reshape(ny * part, 2 * units), "y", 0, 0, tiled=True
        ).reshape(ny, part, 2 * units)
        (copies,) = call(sum_kernel, [(ny, part, 2 * units)], [], 10**6, terms, mib=16)
        hidden_y = lax.all_to_all(
            copies.reshape(ny * part, 2 * units), "y", 0, 0, tiled=True
        ).reshape(ny, part, 2 * units)
        hidden_all = spread(hidden_y, "x", nx)

        pair = (2, ny, nx, part, units)
        factors, factors_send, hidden = call(
            factor_kernel, [pair, pair, (ny, 2, nx, part, units)], [],
            15000 * total * units, core_id, tied(saved, hidden_y),
        )
        factors_other = swap_core(factors_send)
        input_part, hg_send = call(
            input_kernel, [(nz * nx * part, width), (nx, ny, part, units)],
            [(2, ny, nx, part, 2 * units)], 2 * total * units * width,
            hidden_all, factors, both_w, factors_other, w_other, order(60, hidden_all), fetched=5,
        )
        swapped = swap_core(hg_send)
        input_terms = lax.all_to_all(input_part, "z", 0, 0, tiled=True)
        grad_gate, grad_up, grad_down = call(
            functools.partial(weight_kernel, scale),
            [(units, width)] * 3, [(ny, 2, nx, part, units)] * 2, 200 * total * units * width,
            core_id, rows, hidden_all, swapped, factors, factors_send, hidden, mib=62,
        )

        input_terms = tied(input_terms, grad_gate, grad_up, grad_down)
        input_terms = input_terms.reshape(nz, tokens, width)
        in_grad = jnp.sum(input_terms.astype(F32), axis=0).astype(BF)
        return in_grad, grad_gate.T, grad_up.T, grad_down

    return body


def solution(mesh):
    nx = 4 if mesh.shape["row"] >= 16 else 2
    ny, nz = mesh.shape["row"] // nx, mesh.shape["col"] // 2
    grid = Mesh(mesh.devices.reshape(ny, nx, nz, 2), ("y", "x", "z", "core"))
    row, col = ("y", "x"), ("z", "core")
    return jax.shard_map(
        make_body(ny, nx, nz),
        mesh=grid,
        in_specs=(
            P(col, row), P(col, row), P(row, col), P(row, col),
            P(row, col), P(row, col), P(col, row), P(col),
        ),
        out_specs=(P(col, row), P(row, col), P(row, col), P(col, row)),
        check_vma=False,
    )
```
